32 devices in a mesh: groups: 2 (over x), layer: 16 (over z, y, core).
Axes of the slice: x: 2, y: 2, z: 4, core: 2. Of those that a mesh axis runs over, the one named last changes fastest.
Arguments:
- token_ids: int32 [16, 64], P('groups'), parts along dimension 0, may hold values from 0 to 2047
- hidden_pool: bfloat16 [4096, 16384], P('groups', 'layer'), parts along dimension 0, may hold values from -6 to 6
- basis: bfloat16 [16384, 8192], P('layer', 'groups'), parts along dimension 1, may hold values from -0.046875 to 0.046875
- coeffs: bfloat16 [8, 8192, 16384], P(None, 'groups', 'layer'), parts along dimension 1, may hold values from -0.09375 to 0.09375
- targets: bfloat16 [16, 64, 16384], P('groups', None, 'layer'), parts along dimension 0, may hold values from -6 to 6
Outputs:
- residual: float32 [16, 64, 16384], P('groups', None, 'layer'), parts along dimension 0
- basis_grad: float32 [16384, 8192], P('layer', 'groups'), parts along dimension 1
The draws below stay inside these ranges and needn't reach their ends.
There are 2 independent parts, one for each index of `groups`. The reference program is written for one: setup_inputs(seed, part) draws one part's arguments, and reference() takes and returns one part's arrays. A program takes and returns all parts, laid end to end along the dimension named above; each array names one. Nothing has to cross between parts.
All inputs are finite; a program needn't handle non-finite values.
Results may differ from the reference program's by a relative error of at most 0.0041.
Values may be sent and summed in bfloat16 or wider, within the bound.
No kernel may reach another device: no remote copies, remote signals or barrier semaphores. Data moves between devices by JAX's collectives and lax.ppermute only.
A program may use at most 256 MiB of HBM per device.

```python
import jax
import jax.numpy as jnp
from jax import lax

D = 16384
DOUT = 16384
RANK = 4096
LAYERS = 8
TOK = 64
POOL = 2048


def set_ends(entries, rng, least, high):
    longest = entries.shape.index(max(entries.shape))
    spots = []
    for shift in (0, 1):
        where = [jax.random.randint(jax.random.fold_in(rng, axis), (), 0, length) for axis, length in enumerate(entries.shape)]
        where[longest] = (where[longest] + shift) % entries.shape[longest]
        spots.append(tuple(where))
    return entries.at[spots[0]].set(least).at[spots[1]].set(high)


def block_scale(own_key, shape, shards, smallest, largest):
    def one(axis_at, parts):
        steps = jax.random.uniform(jax.random.fold_in(jax.random.fold_in(own_key, 6), axis_at), (parts,), jnp.float32, smallest / len(shards), largest / len(shards))
        return jnp.repeat(jnp.exp(steps), shape[axis_at] // parts).reshape((-1,) + (1,) * (len(shape) - axis_at - 1))

    gain = one(*shards[0])
    for cut in shards[1:]:
        gain = gain * one(*cut)
    return gain


def bell_draw(own_key, dims, spread, limit, split=(), dtype=jnp.bfloat16):
    loudness = block_scale(own_key, dims, split, -0.22, 0.18) if split else 1.0
    drawn = jax.random.normal(own_key, dims, jnp.float32) * spread * loudness
    return jnp.minimum(jnp.maximum(drawn, -limit), limit).astype(dtype)


def setup_inputs(seed: int = 0, part: int = 0) -> dict:
    streams_of = jax.random.split(jax.random.key(seed), 6)
    own_keys = jax.random.split(jax.random.fold_in(streams_of[5], part), 6)
    return {
        "token_ids": set_ends(jax.random.randint(own_keys[0], (LAYERS, TOK), 0, POOL), jax.random.fold_in(own_keys[0], 1), 0, POOL - 1).astype(jnp.int32),
        "hidden_pool": bell_draw(own_keys[1], (POOL, D), 1.0, 6.0, ((1, 16),)),
        "basis": bell_draw(own_keys[2], (D, RANK), D ** -0.5, 0.046875, ((0, 16),)),
        "coeffs": bell_draw(own_keys[3], (LAYERS, RANK, DOUT), RANK ** -0.5, 0.09375, ((2, 16),)),
        "targets": bell_draw(own_keys[4], (LAYERS, TOK, DOUT), 1.0, 6.0, ((2, 16),)),
    }


def reference(token_ids, hidden_pool, basis, coeffs, targets):
    row_count = LAYERS * TOK
    inputs = jnp.take(hidden_pool, token_ids.reshape(-1).astype(jnp.int32), axis=0)
    proj = jnp.dot(inputs, basis, preferred_element_type=jnp.float32).astype(jnp.bfloat16)
    proj = proj.reshape(LAYERS, TOK, RANK)

    def one_layer(layer_args):
        proj_layer, coeff_layer, target_layer = layer_args
        predicted = jnp.dot(proj_layer, coeff_layer, preferred_element_type=jnp.float32)
        resid = target_layer.astype(jnp.float32) - predicted
        back_layer = jnp.dot(resid.astype(jnp.bfloat16), coeff_layer.T, preferred_element_type=jnp.float32)
        return resid, back_layer.astype(jnp.bfloat16)

    residual, back = lax.map(one_layer, (proj, coeffs, targets))
    grad = jnp.dot(inputs.T, back.reshape(row_count, RANK), preferred_element_type=jnp.float32)
    return residual, grad * (-1.0 / TOK)
```

```python
import functools
import math

import jax
import jax.numpy as jnp
from jax import lax
from jax.experimental import pallas as pl
from jax.experimental.pallas import tpu as pltpu
from jax.sharding import PartitionSpec as P

X_MAX = 6.0
BASIS_MAX = 0.046875
F32 = jnp.float32
BF16 = jnp.bfloat16
F16 = jnp.float16
IN_VMEM = pl.BlockSpec(memory_space=pltpu.MemorySpace.VMEM)
IN_SMEM = pl.BlockSpec(memory_space=pltpu.MemorySpace.SMEM)
IN_HBM = pl.BlockSpec(memory_space=pltpu.MemorySpace.HBM)
MIB = 2**20


def params(mib):
    return pltpu.CompilerParams(vmem_limit_bytes=mib * MIB)


def cost(flops, moved):
    return pl.CostEstimate(flops=flops, bytes_accessed=moved, transcendentals=0)


def block(ref, i, size):
    return pl.ds(pl.multiple_of(ref[i] * size, size), size)


def join(value, mark):
    return pl.pallas_call(
        lambda value_ref, mark_ref, out_ref: None,
        out_shape=jax.ShapeDtypeStruct(value.shape, value.dtype),
        in_specs=[IN_VMEM, IN_VMEM],
        out_specs=IN_VMEM,
        input_output_aliases={0: 0},
        compiler_params=params(2),
        name="join",
    )(value, mark)


def start_body(cols, kb, idx_ref, hot_ref, pool_ref, basis_ref, x_ref, tiles_ref, sems):
    n = tiles_ref.shape[0]

    def tile(i):
        return pltpu.make_async_copy(basis_ref.at[:, block(idx_ref, i, kb)], tiles_ref.at[i], sems.at[i])

    for i in range(n):
        tile(i).start()

    @pl.loop(0, x_ref.shape[1] // cols)
    def _(i):
        window = pl.ds(pl.multiple_of(i * cols, cols), cols)
        x_ref[:, window] = jnp.dot(
            hot_ref[...], pool_ref[:, window], preferred_element_type=F32
        ).astype(BF16)

    @pl.loop(0, n)
    def _(i):
        tile(i).wait()


def start(idx, ids, pool, basis, kb):
    rows = ids.shape[0]
    pool_rows, depth = pool.shape
    n = idx.shape[0]
    hot = (ids == lax.broadcasted_iota(jnp.int32, (rows, pool_rows), 1)).astype(BF16)
    return pl.pallas_call(
        functools.partial(start_body, 256, kb),
        out_shape=(
            jax.ShapeDtypeStruct((rows, depth), BF16),
            jax.ShapeDtypeStruct((n, depth, kb), BF16),
        ),
        in_specs=[IN_SMEM, IN_VMEM, IN_VMEM, IN_HBM],
        out_specs=(IN_VMEM, IN_VMEM),
        scratch_shapes=[pltpu.SemaphoreType.DMA((n,))],
        compiler_params=params(36),
        cost_estimate=cost(2 * rows * pool_rows * depth, pool_rows * depth * 2),
        name="start",
    )(idx, hot, pool, basis)


def project_body(first, sizes, x_ref, tiles_ref, mark_ref, *outs):
    base = first
    for out, size in zip(outs, sizes):

        @pl.loop(0, size)
        def _(j, base=base, out=out):
            out[j] = jnp.dot(x_ref[...], tiles_ref[base + j], preferred_element_type=F32)

        base += size


def project(first, sizes, x, tiles, mark):
    rows, depth = x.shape
    kb = tiles.shape[2]
    n = sum(sizes)
    return pl.pallas_call(
        functools.partial(project_body, first, sizes),
        out_shape=tuple(jax.ShapeDtypeStruct((size, rows, kb), F32) for size in sizes),
        in_specs=[IN_VMEM, IN_VMEM, IN_VMEM],
        out_specs=(IN_VMEM,) * len(sizes),
        compiler_params=params(8),
        cost_estimate=cost(2 * n * rows * depth * kb, n * depth * kb * 2),
        name="project",
    )(x, tiles, mark)


def finish(keep, other, to_right, to_left):
    _, kb, rows = keep.shape

    def body(keep_ref, other_ref, right_ref, left_ref, out_ref):
        total = keep_ref[0] + other_ref[0] + right_ref[...].astype(F32) + left_ref[...].astype(F32)
        out_ref[...] = total.T.astype(BF16)

    return pl.pallas_call(
        body,
        out_shape=jax.ShapeDtypeStruct((rows, kb), BF16),
        in_specs=[IN_VMEM] * 4,
        out_specs=IN_VMEM,
        compiler_params=params(8),
        name="finish",
    )(keep, other, to_right, to_left)


def coeff_copy(idx_ref, coeff_ref, buf, sems, kb, l, i):
    return pltpu.make_async_copy(
        coeff_ref.at[l, block(idx_ref, i, kb), :], buf.at[l, pl.ds(i * kb, kb), :], sems.at[l, i]
    )


def start_coeffs(idx_ref, coeff_ref, buf, sems, n, kb):
    @pl.loop(0, buf.shape[0])
    def _(l):
        for i in range(n):
            coeff_copy(idx_ref, coeff_ref, buf, sems, kb, l, i).start()


def wait_coeffs(idx_ref, coeff_ref, buf, sems, n, kb, l):
    for i in range(n):
        coeff_copy(idx_ref, coeff_ref, buf, sems, kb, l, i).wait()


def rows_of(l, size):
    return pl.ds(pl.multiple_of(l * size, size), size)


def wide(pieces, span):
    return jnp.concatenate([piece[span, :] for piece in pieces], axis=1)


def predict_body(n, first, idx_ref, coeff_ref, *refs):
    pieces, rest = refs[:n], refs[n:]
    if first:
        out_ref, mark_ref, buf, sems = rest
    else:
        acc_ref, out_ref, mark_ref, buf, sems = rest
    layer_count = buf.shape[0]
    mark_ref[...] = jnp.zeros_like(mark_ref)
    rows, kb = pieces[0].shape
    toks = rows // layer_count
    start_coeffs(idx_ref, coeff_ref, buf, sems, n, kb)

    @pl.loop(0, layer_count)
    def _(l):
        span = rows_of(l, toks)
        wait_coeffs(idx_ref, coeff_ref, buf, sems, n, kb, l)
        part = jnp.dot(wide(pieces, span), buf[l], preferred_element_type=F32)
        out_ref[span, :] = part if first else acc_ref[span, :] + part


def coeff_scratch(coeffs, n, kb):
    layer_count, _, width = coeffs.shape
    return [pltpu.VMEM((layer_count, n * kb, width), BF16), pltpu.SemaphoreType.DMA((layer_count, n))]


def predict(idx, coeffs, pieces, acc):
    n = len(pieces)
    rows, kb = pieces[0].shape
    layer_count, _, width = coeffs.shape
    first = acc is None
    return pl.pallas_call(
        functools.partial(predict_body, n, first),
        out_shape=(jax.ShapeDtypeStruct((rows, width), F32), jax.ShapeDtypeStruct((8, 128), F32)),
        in_specs=[IN_SMEM, IN_HBM] + [IN_VMEM] * (n + (not first)),
        out_specs=(IN_VMEM, IN_VMEM),
        input_output_aliases={} if first else {n + 2: 0},
        scratch_shapes=coeff_scratch(coeffs, n, kb),
        compiler_params=params(4 * n + 3),
        cost_estimate=cost(8 * n * rows * kb * width, layer_count * n * kb * width * 2),
        name="predict",
    )(idx, coeffs, *pieces, *([] if first else [acc]))


def back_blocks(low, buf, l, keep_ref, send_ref, toks):
    m, kb, _ = keep_ref.shape
    parts = [
        lax.dot_general(
            buf[l + j],
            low[j * toks : (j + 1) * toks, :],
            (((1,), (1,)), ((), ())),
            preferred_element_type=F32,
        )
        for j in range(2)
    ]
    both = jnp.concatenate(parts, axis=1)
    lanes = pl.ds(pl.multiple_of(l * toks, 2 * toks), 2 * toks)
    for i in range(m):
        keep_ref[i, :, lanes] = both[i * kb : (i + 1) * kb, :]
        send_ref[i, :, lanes] = both[(m + i) * kb : (m + i + 1) * kb, :]


def residual_body(n, idx_ref, coeff_ref, *refs):
    pieces, (target_ref, acc_ref, res_ref, low_ref, keep_ref, send_ref, buf, sems) = refs[:n], refs[n:]
    layer_count = buf.shape[0]
    rows, kb = pieces[0].shape
    toks = rows // layer_count
    start_coeffs(idx_ref, coeff_ref, buf, sems, n, kb)

    @pl.loop(0, layer_count, step=2)
    def _(l):
        for j in range(2):
            span = rows_of(l + j, toks)
            wait_coeffs(idx_ref, coeff_ref, buf, sems, n, kb, l + j)
            part = jnp.dot(wide(pieces, span), buf[l + j], preferred_element_type=F32)
            res = target_ref[l + j].astype(F32) - (acc_ref[span, :] + part)
            res_ref[l + j] = res
            low_ref[span, :] = res.astype(BF16)
        pair = pl.ds(pl.multiple_of(l * toks, 2 * toks), 2 * toks)
        back_blocks(low_ref[pair, :], buf, l, keep_ref, send_ref, toks)


def residuals(idx, coeffs, pieces, targets, acc):
    n = len(pieces)
    rows, kb = pieces[0].shape
    layer_count, _, width = coeffs.shape
    half = jax.ShapeDtypeStruct((n // 2, kb, rows), F32)
    return pl.pallas_call(
        functools.partial(residual_body, n),
        out_shape=(
            jax.ShapeDtypeStruct(targets.shape, F32),
            jax.ShapeDtypeStruct((rows, width), BF16),
            half,
            half,
        ),
        in_specs=[IN_SMEM, IN_HBM] + [IN_VMEM] * (n + 2),
        out_specs=(IN_VMEM,) * 4,
        scratch_shapes=coeff_scratch(coeffs, n, kb),
        compiler_params=params(4 * n + 3),
        cost_estimate=cost(16 * n * rows * kb * width, layer_count * n * kb * width * 2),
        name="residuals",
    )(idx, coeffs, *pieces, targets, acc)


def backward_body(n, idx_ref, coeff_ref, low_ref, mark_ref, keep_ref, send_ref, buf, sems):
    layer_count = buf.shape[0]
    kb = keep_ref.shape[1]
    toks = low_ref.shape[0] // layer_count
    start_coeffs(idx_ref, coeff_ref, buf, sems, n, kb)

    @pl.loop(0, layer_count, step=2)
    def _(l):
        for j in range(2):
            wait_coeffs(idx_ref, coeff_ref, buf, sems, n, kb, l + j)
        pair = pl.ds(pl.multiple_of(l * toks, 2 * toks), 2 * toks)
        back_blocks(low_ref[pair, :], buf, l, keep_ref, send_ref, toks)


def backward(idx, coeffs, low, mark, kb):
    n = idx.shape[0]
    rows = low.shape[0]
    layer_count, _, width = coeffs.shape
    half = jax.ShapeDtypeStruct((n // 2, kb, rows), F32)
    return pl.pallas_call(
        functools.partial(backward_body, n),
        out_shape=(half, half),
        in_specs=[IN_SMEM, IN_HBM, IN_VMEM, IN_VMEM],
        out_specs=(IN_VMEM,) * 2,
        scratch_shapes=coeff_scratch(coeffs, n, kb),
        compiler_params=params(4 * n + 3),
        cost_estimate=cost(8 * n * rows * kb * width, layer_count * n * kb * width * 2),
        name="backward",
    )(idx, coeffs, low, mark)


def gradient_body(n, scale, first, idx_ref, xt_ref, *refs):
    pieces, (out_ref, mark_ref, buf, sems) = refs[:n], refs[n + (not first) :]
    mark_ref[...] = jnp.zeros_like(mark_ref)
    kb = buf.shape[2]
    depth = buf.shape[1]
    copies = []
    for i in range(n):

        @pl.loop(0, 2)
        def _(r, i=i):
            span = rows_of(r, depth // 2)
            buf[i, span, :] = jnp.dot(xt_ref[span, :], pieces[i][...], preferred_element_type=F32) * scale

        copies.append(
            pltpu.make_async_copy(buf.at[i], out_ref.at[:, block(idx_ref, i, kb)], sems.at[i])
        )
        copies[-1].start()
    for copy in copies:
        copy.wait()


def gradient(idx, xt, pieces, grad, width, scale):
    n = len(pieces)
    kb = pieces[0].shape[1]
    depth, rows = xt.shape
    first = grad is None
    return pl.pallas_call(
        functools.partial(gradient_body, n, scale, first),
        out_shape=(jax.ShapeDtypeStruct((depth, width), F32), jax.ShapeDtypeStruct((8, 128), F32)),
        in_specs=[IN_SMEM] + [IN_VMEM] * (n + 1) + [IN_HBM] * (not first),
        out_specs=(IN_HBM, IN_VMEM),
        input_output_aliases={} if first else {n + 2: 0},
        scratch_shapes=[pltpu.VMEM((n, depth, kb), F32), pltpu.SemaphoreType.DMA((n,))],
        compiler_params=params(16),
        cost_estimate=cost(2 * n * depth * rows * kb, n * depth * kb * 4),
        name="gradient",
    )(idx, xt, *pieces, *([] if first else [grad]))


def plain(token_ids, hidden_pool, basis, coeffs, targets):
    layer_count, tok_count = token_ids.shape
    x_local = jnp.take(hidden_pool, token_ids.reshape(-1), axis=0)
    share = lax.psum_scatter(
        lax.dot_general(basis, x_local, (((0,), (1,)), ((), ())), preferred_element_type=F32),
        "layer",
        scatter_dimension=0,
        tiled=True,
    ).astype(BF16)
    piece = lax.all_gather(share, "layer", axis=0, tiled=True)
    shaped = piece.reshape(piece.shape[0], layer_count, tok_count)
    predicted = jnp.einsum("kls,lko->lso", shaped, coeffs, preferred_element_type=F32)
    residual = targets.astype(F32) - predicted
    summed = jnp.einsum("lko,lso->kls", coeffs, residual.astype(BF16), preferred_element_type=F32)
    summed = summed.reshape(basis.shape[1], -1)
    back = lax.psum_scatter(summed, "layer", scatter_dimension=0, tiled=True).astype(BF16)
    back = lax.all_gather(back, "layer", axis=0, tiled=True)
    product = lax.dot_general(x_local, back, (((0,), (1,)), ((), ())), preferred_element_type=F32)
    return residual, product * (-1.0 / tok_count)


def staged(zn, token_ids, hidden_pool, basis, coeffs, targets):
    chips = 2 * zn
    tok_count = token_ids.shape[1]
    rank = basis.shape[1]
    kb = rank // (2 * chips)
    me = lax.axis_index("layer")
    core, y, z = me % 2, (me // 2) % 2, me // 4
    place = jnp.where(y == 0, z, chips - 1 - z)
    order = [2 * z for z in range(zn)] + [2 * z + 1 for z in reversed(range(zn))]

    def turn(step):
        return [
            (2 * order[i] + c, 2 * order[(i + step) % chips] + c) for i in range(chips) for c in range(2)
        ]

    right, left = turn(1), turn(-1)
    across = [(i, i ^ 1) for i in range(2 * chips)]

    def send(a, pairs):
        return lax.ppermute(a, "layer", pairs)

    def index(half, i):
        return (core ^ half) * chips + (place + i) % chips

    far = chips // 2
    rounds = [[far]] + [[i, chips - i] for i in range(far - 1, 0, -1)] + [[0]]

    def both(items):
        return jnp.stack([index(h, i) for h in range(2) for i in items]).astype(jnp.int32)

    def scatter_sum(parts, wire, scale, last):
        keeps, others = [], []

        def mine(r, j):
            return (keeps[r][j] + others[r][j]) * scale

        def blocks(r, mark):
            keep, out = parts[r](mark)
            keeps.append(keep)
            return out

        def swap(out, mark):
            others.append(send(out if mark is None else join(out, mark), across))

        def corner(message):
            return message[:8, :128].astype(F32)

        swap(blocks(0, None), None)
        out = blocks(1, None)
        first = mine(0, 0).astype(wire)
        cut = first.shape[0] // 2
        to_right, to_left = send(first[:cut], right), send(first[cut:], left)
        for r in range(1, far):
            mark = corner(first)
            swap(out, mark)
            out = blocks(r + 1, mark)
            a, b = mine(r, 0), mine(r, 1)
            if r == 1:
                a = jnp.concatenate([a[:cut] + to_right.astype(F32), a[cut:]])
                b = jnp.concatenate([b[:cut], b[cut:] + to_left.astype(F32)])
            else:
                a, b = a + to_right.astype(F32), b + to_left.astype(F32)
            first, second = a.astype(wire), b.astype(wire)
            to_right, to_left = send(first, right), send(second, left)
        swap(out, corner(first))
        return last(keeps[far], others[far], to_right, to_left)

    def gather(own, use, lag):
        a, b = send(own, right), send(own, left)
        came = [([(0, 0)], [own])]
        waiting = [([(1, 0)], [send(own, across)])]
        cut = own.shape[0] // 2
        for i in range(1, far):
            if not lag:
                came, waiting = came + waiting, []
            mark = use(sum([c[0] for c in came], []), sum([c[1] for c in came], []))
            came, waiting = waiting, []
            a = join(a, mark)
            places, got = [chips - i, i], [a, b]
            if i < far - 1:
                a, b = send(a, right), send(b, left)
            else:
                a, b = send(a[:cut], right), send(b[cut:], left)
            came.append(([(0, p) for p in places], got))
            waiting.append(([(1, p) for p in places], [send(piece, across) for piece in got]))
        came = came + waiting
        mark = use(sum([c[0] for c in came], []), sum([c[1] for c in came], []))
        last = jnp.concatenate([join(a, mark), b])
        return [(0, far), (1, far)], [last, send(last, across)]

    def where(items):
        return jnp.stack([index(h, i) for h, i in items]).astype(jnp.int32)

    features = basis.shape[0] * 2 * chips
    wire_scale = 2.0 ** math.floor(math.log2(60000.0 / (X_MAX * BASIS_MAX * features)))
    listed = [(h, i) for r in rounds for h in range(2) for i in r]
    x, tiles = start(where(listed), token_ids.reshape(-1, 1), hidden_pool, basis, kb)

    def projected(r):
        first = sum(2 * len(items) for items in rounds[:r])
        return lambda mark: project(first, (len(rounds[r]),) * 2, x, tiles, x if mark is None else mark)

    def rounded(keep, other, to_right, to_left):
        total = (keep[0] + other[0]) * wire_scale + to_right.astype(F32) + to_left.astype(F32)
        return (total * (1.0 / wire_scale)).astype(BF16)

    own = scatter_sum([projected(r) for r in range(far + 1)], F16, wire_scale, rounded)

    state = {"acc": None, "grad": None}

    def use_forward(items, blocks):
        state["acc"], mark = predict(where(items), coeffs, blocks, state["acc"])
        return mark

    items, last = gather(own, use_forward, True)
    res, low, keep, out = residuals(where(items), coeffs, last, targets, state["acc"])

    def backed(r):
        return lambda mark: backward(both(rounds[r]), coeffs, low, keep if mark is None else mark, kb)

    parts = [lambda mark: (keep, out)] + [backed(r) for r in range(1, far + 1)]
    own = scatter_sum(parts, BF16, 1.0, finish)
    xt = x.T

    def use_back(items, blocks):
        state["grad"], mark = gradient(where(items), xt, blocks, state["grad"], rank, -1.0 / tok_count)
        return mark

    use_back(*gather(own, use_back, False))
    return res, state["grad"]


def solution(mesh):
    placed = (
        P("groups", None),
        P("groups", "layer"),
        P("layer", "groups"),
        P(None, "groups", "layer"),
        P("groups", None, "layer"),
    )
    count = mesh.shape["layer"]
    body = functools.partial(staged, 4) if count == 16 else plain
    return jax.shard_map(
        body,
        mesh=mesh,
        in_specs=placed,
        out_specs=(P("groups", None, "layer"), P("layer", "groups")),
        check_vma=False,
    )
```

```python
import functools
import math

import jax
import jax.numpy as jnp
from jax import lax
from jax.experimental import pallas as pl
from jax.experimental.pallas import tpu as pltpu
from jax.sharding import PartitionSpec as P

X_MAX = 6.0
BASIS_MAX = 0.046875
F32 = jnp.float32
BF16 = jnp.bfloat16
F16 = jnp.float16
IN_VMEM = pl.BlockSpec(memory_space=pltpu.MemorySpace.VMEM)
IN_SMEM = pl.BlockSpec(memory_space=pltpu.MemorySpace.SMEM)
IN_HBM = pl.BlockSpec(memory_space=pltpu.MemorySpace.HBM)
MIB = 2**20


def params(mib):
    return pltpu.CompilerParams(vmem_limit_bytes=mib * MIB)


def cost(flops, moved):
    return pl.CostEstimate(flops=flops, bytes_accessed=moved, transcendentals=0)


def block(ref, i, size):
    return pl.ds(pl.multiple_of(ref[i] * size, size), size)


def join(value, mark):
    return pl.pallas_call(
        lambda value_ref, mark_ref, out_ref: None,
        out_shape=jax.ShapeDtypeStruct(value.shape, value.dtype),
        in_specs=[IN_VMEM, IN_VMEM],
        out_specs=IN_VMEM,
        input_output_aliases={0: 0},
        compiler_params=params(2),
        name="join",
    )(value, mark)


def start_body(cols, kb, idx_ref, hot_ref, pool_ref, basis_ref, x_ref, tiles_ref, sems):
    n = tiles_ref.shape[0]

    def tile(i):
        return pltpu.make_async_copy(basis_ref.at[:, block(idx_ref, i, kb)], tiles_ref.at[i], sems.at[i])

    for i in range(n):
        tile(i).start()

    @pl.loop(0, x_ref.shape[1] // cols)
    def _(i):
        window = pl.ds(pl.multiple_of(i * cols, cols), cols)
        x_ref[:, window] = jnp.dot(
            hot_ref[...], pool_ref[:, window], preferred_element_type=F32
        ).astype(BF16)

    @pl.loop(0, n)
    def _(i):
        tile(i).wait()


def start(idx, ids, pool, basis, kb):
    rows = ids.shape[0]
    pool_rows, depth = pool.shape
    n = idx.shape[0]
    hot = (ids == lax.broadcasted_iota(jnp.int32, (rows, pool_rows), 1)).astype(BF16)
    return pl.pallas_call(
        functools.partial(start_body, 256, kb),
        out_shape=(
            jax.ShapeDtypeStruct((rows, depth), BF16),
            jax.ShapeDtypeStruct((n, depth, kb), BF16),
        ),
        in_specs=[IN_SMEM, IN_VMEM, IN_VMEM, IN_HBM],
        out_specs=(IN_VMEM, IN_VMEM),
        scratch_shapes=[pltpu.SemaphoreType.DMA((n,))],
        compiler_params=params(36),
        cost_estimate=cost(2 * rows * pool_rows * depth, pool_rows * depth * 2),
        name="start",
    )(idx, hot, pool, basis)


def project_body(first, sizes, x_ref, tiles_ref, mark_ref, *outs):
    base = first
    for out, size in zip(outs, sizes):

        @pl.loop(0, size)
        def _(j, base=base, out=out):
            out[j] = jnp.dot(x_ref[...], tiles_ref[base + j], preferred_element_type=F32)

        base += size


def project(first, sizes, x, tiles, mark):
    rows, depth = x.shape
    kb = tiles.shape[2]
    n = sum(sizes)
    return pl.pallas_call(
        functools.partial(project_body, first, sizes),
        out_shape=tuple(jax.ShapeDtypeStruct((size, rows, kb), F32) for size in sizes),
        in_specs=[IN_VMEM, IN_VMEM, IN_VMEM],
        out_specs=(IN_VMEM,) * len(sizes),
        compiler_params=params(8),
        cost_estimate=cost(2 * n * rows * depth * kb, n * depth * kb * 2),
        name="project",
    )(x, tiles, mark)


def finish(keep, other, to_right, to_left):
    _, kb, rows = keep.shape

    def body(keep_ref, other_ref, right_ref, left_ref, out_ref):
        total = keep_ref[0] + other_ref[0] + right_ref[...].astype(F32) + left_ref[...].astype(F32)
        out_ref[...] = total.T.astype(BF16)

    return pl.pallas_call(
        body,
        out_shape=jax.ShapeDtypeStruct((rows, kb), BF16),
        in_specs=[IN_VMEM] * 4,
        out_specs=IN_VMEM,
        compiler_params=params(8),
        name="finish",
    )(keep, other, to_right, to_left)


def coeff_copy(idx_ref, coeff_ref, buf, sems, kb, l, i):
    return pltpu.make_async_copy(
        coeff_ref.at[l, block(idx_ref, i, kb), :], buf.at[l, pl.ds(i * kb, kb), :], sems.at[l, i]
    )


def start_coeffs(idx_ref, coeff_ref, buf, sems, n, kb):
    @pl.loop(0, buf.shape[0])
    def _(l):
        for i in range(n):
            coeff_copy(idx_ref, coeff_ref, buf, sems, kb, l, i).start()


def wait_coeffs(idx_ref, coeff_ref, buf, sems, n, kb, l):
    for i in range(n):
        coeff_copy(idx_ref, coeff_ref, buf, sems, kb, l, i).wait()


def rows_of(l, size):
    return pl.ds(pl.multiple_of(l * size, size), size)


def wide(pieces, span):
    return jnp.concatenate([piece[span, :] for piece in pieces], axis=1)


def predicted(l, span, pieces, copied, buf, held, held_refs):
    total = None
    if copied:
        total = jnp.dot(wide(pieces[:copied], span), buf[l], preferred_element_type=F32)
    for k in range(held):
        pair = pieces[copied + 2 * k : copied + 2 * k + 2]
        part = jnp.dot(wide(pair, span), held_refs[k][l], preferred_element_type=F32)
        total = part if total is None else total + part
    return total


def predict_body(n, held, first, idx_ref, coeff_ref, *refs):
    count = n + 2 * held
    pieces, held_refs, rest = refs[:count], refs[count : count + held], refs[count + held :]
    if first:
        out_ref, mark_ref, buf, sems = rest
    else:
        acc_ref, out_ref, mark_ref, buf, sems = rest
    layer_count = buf.shape[0]
    mark_ref[...] = jnp.zeros_like(mark_ref)
    rows, kb = pieces[0].shape
    toks = rows // layer_count
    start_coeffs(idx_ref, coeff_ref, buf, sems, n, kb)

    @pl.loop(0, layer_count)
    def _(l):
        span = rows_of(l, toks)
        wait_coeffs(idx_ref, coeff_ref, buf, sems, n, kb, l)
        part = predicted(l, span, pieces, n, buf, held, held_refs)
        out_ref[span, :] = part if first else acc_ref[span, :] + part


def coeff_scratch(coeffs, n, kb):
    layer_count, _, width = coeffs.shape
    return [pltpu.VMEM((layer_count, n * kb, width), BF16), pltpu.SemaphoreType.DMA((layer_count, n))]


def predict(idx, coeffs, pieces, tiles, acc):
    n = idx.shape[0]
    held = len(tiles)
    rows, kb = pieces[0].shape
    layer_count, _, width = coeffs.shape
    first = acc is None
    inputs = len(pieces) + held
    return pl.pallas_call(
        functools.partial(predict_body, n, held, first),
        out_shape=(jax.ShapeDtypeStruct((rows, width), F32), jax.ShapeDtypeStruct((8, 128), F32)),
        in_specs=[IN_SMEM, IN_HBM] + [IN_VMEM] * (inputs + (not first)),
        out_specs=(IN_VMEM, IN_VMEM),
        input_output_aliases={} if first else {inputs + 2: 0},
        scratch_shapes=coeff_scratch(coeffs, n, kb),
        compiler_params=params(4 * n + 3),
        cost_estimate=cost(8 * len(pieces) * rows * kb * width, layer_count * n * kb * width * 2),
        name="predict",
    )(idx, coeffs, *pieces, *tiles, *([] if first else [acc]))


def hold_body(n, kb, idx_ref, coeff_ref, after_ref, tiles_ref, mark_ref, sems):
    mark_ref[...] = jnp.zeros_like(mark_ref)
    start_coeffs(idx_ref, coeff_ref, tiles_ref, sems, n, kb)

    @pl.loop(0, tiles_ref.shape[0])
    def _(l):
        wait_coeffs(idx_ref, coeff_ref, tiles_ref, sems, n, kb, l)


def hold(idx, coeffs, kb, mark):
    n = idx.shape[0]
    layer_count, _, width = coeffs.shape
    return pl.pallas_call(
        functools.partial(hold_body, n, kb),
        out_shape=(
            jax.ShapeDtypeStruct((layer_count, n * kb, width), BF16),
            jax.ShapeDtypeStruct((8, 128), F32),
        ),
        in_specs=[IN_SMEM, IN_HBM, IN_VMEM],
        out_specs=(IN_VMEM, IN_VMEM),
        scratch_shapes=coeff_scratch(coeffs, n, kb)[1:],
        compiler_params=params(12),
        cost_estimate=cost(0, layer_count * n * kb * width * 2),
        name="hold",
    )(idx, coeffs, mark)


def back_blocks(low, tiles, l, outs, toks):
    kb = outs[0].shape[0]
    parts = [
        lax.dot_general(
            tiles[l + j],
            low[j * toks : (j + 1) * toks, :],
            (((1,), (1,)), ((), ())),
            preferred_element_type=F32,
        )
        for j in range(2)
    ]
    both = jnp.concatenate(parts, axis=1)
    lanes = pl.ds(pl.multiple_of(l * toks, 2 * toks), 2 * toks)
    for i, out in enumerate(outs):
        out[:, lanes] = both[i * kb : (i + 1) * kb, :]


def residual_body(a_ref, b_ref, tiles_ref, target_ref, acc_ref, res_ref, low_ref, keep_ref, send_ref):
    layer_count, toks, _ = target_ref.shape

    @pl.loop(0, layer_count, step=2)
    def _(l):
        for j in range(2):
            span = rows_of(l + j, toks)
            part = predicted(l + j, span, (a_ref, b_ref), 0, None, 1, (tiles_ref,))
            res = target_ref[l + j].astype(F32) - (acc_ref[span, :] + part)
            res_ref[l + j] = res
            low_ref[span, :] = res.astype(BF16)
        pair = pl.ds(pl.multiple_of(l * toks, 2 * toks), 2 * toks)
        back_blocks(low_ref[pair, :], tiles_ref, l, [keep_ref.at[0], send_ref.at[0]], toks)


def residuals(pieces, tiles, targets, acc):
    rows, kb = pieces[0].shape
    layer_count, _, width = targets.shape
    half = jax.ShapeDtypeStruct((1, kb, rows), F32)
    return pl.pallas_call(
        residual_body,
        out_shape=(
            jax.ShapeDtypeStruct(targets.shape, F32),
            jax.ShapeDtypeStruct((rows, width), BF16),
            half,
            half,
        ),
        in_specs=[IN_VMEM] * 5,
        out_specs=(IN_VMEM,) * 4,
        compiler_params=params(8),
        cost_estimate=cost(32 * rows * kb * width, tiles.size * 2),
        name="residuals",
    )(*pieces, tiles, targets, acc)


def backward_body(n, idx_ref, coeff_ref, low_ref, mark_ref, keep_ref, send_ref, buf, sems):
    layer_count = buf.shape[0]
    m, kb, _ = keep_ref.shape
    toks = low_ref.shape[0] // layer_count
    start_coeffs(idx_ref, coeff_ref, buf, sems, n, kb)

    @pl.loop(0, layer_count, step=2)
    def _(l):
        for j in range(2):
            wait_coeffs(idx_ref, coeff_ref, buf, sems, n, kb, l + j)
        pair = pl.ds(pl.multiple_of(l * toks, 2 * toks), 2 * toks)
        outs = [keep_ref.at[i] for i in range(m)] + [send_ref.at[i] for i in range(m)]
        back_blocks(low_ref[pair, :], buf, l, outs, toks)


def backward(idx, coeffs, low, mark, kb):
    n = idx.shape[0]
    rows = low.shape[0]
    layer_count, _, width = coeffs.shape
    half = jax.ShapeDtypeStruct((n // 2, kb, rows), F32)
    return pl.pallas_call(
        functools.partial(backward_body, n),
        out_shape=(half, half),
        in_specs=[IN_SMEM, IN_HBM, IN_VMEM, IN_VMEM],
        out_specs=(IN_VMEM,) * 2,
        scratch_shapes=coeff_scratch(coeffs, n, kb),
        compiler_params=params(4 * n + 3),
        cost_estimate=cost(8 * n * rows * kb * width, layer_count * n * kb * width * 2),
        name="backward",
    )(idx, coeffs, low, mark)


def backward_held_body(layer_count, low_ref, mark_ref, *refs):
    tiles, (keep_ref, send_ref) = refs[:-2], refs[-2:]
    toks = low_ref.shape[0] // layer_count

    @pl.loop(0, layer_count, step=2)
    def _(l):
        pair = pl.ds(pl.multiple_of(l * toks, 2 * toks), 2 * toks)
        for i, tile in enumerate(tiles):
            back_blocks(low_ref[pair, :], tile, l, [keep_ref.at[i], send_ref.at[i]], toks)


def backward_held(tiles, low, mark, kb):
    m = len(tiles)
    rows = low.shape[0]
    layer_count, _, width = tiles[0].shape
    half = jax.ShapeDtypeStruct((m, kb, rows), F32)
    return pl.pallas_call(
        functools.partial(backward_held_body, layer_count),
        out_shape=(half, half),
        in_specs=[IN_VMEM] * (m + 2),
        out_specs=(IN_VMEM,) * 2,
        compiler_params=params(8),
        cost_estimate=cost(16 * m * rows * kb * width, m * tiles[0].size * 2),
        name="backward_held",
    )(low, mark, *tiles)


def gradient_body(n, scale, first, idx_ref, xt_ref, *refs):
    pieces, (out_ref, mark_ref, buf, sems) = refs[:n], refs[n + (not first) :]
    mark_ref[...] = jnp.zeros_like(mark_ref)
    kb = buf.shape[2]
    depth = buf.shape[1]
    copies = []
    for i in range(n):

        @pl.loop(0, 2)
        def _(r, i=i):
            span = rows_of(r, depth // 2)
            buf[i, span, :] = jnp.dot(xt_ref[span, :], pieces[i][...], preferred_element_type=F32) * scale

        copies.append(
            pltpu.make_async_copy(buf.at[i], out_ref.at[:, block(idx_ref, i, kb)], sems.at[i])
        )
        copies[-1].start()
    for copy in copies:
        copy.wait()


def gradient(idx, xt, pieces, grad, width, scale):
    n = len(pieces)
    kb = pieces[0].shape[1]
    depth, rows = xt.shape
    first = grad is None
    return pl.pallas_call(
        functools.partial(gradient_body, n, scale, first),
        out_shape=(jax.ShapeDtypeStruct((depth, width), F32), jax.ShapeDtypeStruct((8, 128), F32)),
        in_specs=[IN_SMEM] + [IN_VMEM] * (n + 1) + [IN_HBM] * (not first),
        out_specs=(IN_HBM, IN_VMEM),
        input_output_aliases={} if first else {n + 2: 0},
        scratch_shapes=[pltpu.VMEM((n, depth, kb), F32), pltpu.SemaphoreType.DMA((n,))],
        compiler_params=params(16),
        cost_estimate=cost(2 * n * depth * rows * kb, n * depth * kb * 4),
        name="gradient",
    )(idx, xt, *pieces, *([] if first else [grad]))


def plain(token_ids, hidden_pool, basis, coeffs, targets):
    layer_count, tok_count = token_ids.shape
    x_local = jnp.take(hidden_pool, token_ids.reshape(-1), axis=0)
    share = lax.psum_scatter(
        lax.dot_general(basis, x_local, (((0,), (1,)), ((), ())), preferred_element_type=F32),
        "layer",
        scatter_dimension=0,
        tiled=True,
    ).astype(BF16)
    piece = lax.all_gather(share, "layer", axis=0, tiled=True)
    shaped = piece.reshape(piece.shape[0], layer_count, tok_count)
    predicted = jnp.einsum("kls,lko->lso", shaped, coeffs, preferred_element_type=F32)
    residual = targets.astype(F32) - predicted
    summed = jnp.einsum("lko,lso->kls", coeffs, residual.astype(BF16), preferred_element_type=F32)
    summed = summed.reshape(basis.shape[1], -1)
    back = lax.psum_scatter(summed, "layer", scatter_dimension=0, tiled=True).astype(BF16)
    back = lax.all_gather(back, "layer", axis=0, tiled=True)
    product = lax.dot_general(x_local, back, (((0,), (1,)), ((), ())), preferred_element_type=F32)
    return residual, product * (-1.0 / tok_count)


def staged(zn, token_ids, hidden_pool, basis, coeffs, targets):
    chips = 2 * zn
    tok_count = token_ids.shape[1]
    rank = basis.shape[1]
    kb = rank // (2 * chips)
    me = lax.axis_index("layer")
    core, y, z = me % 2, (me // 2) % 2, me // 4
    place = jnp.where(y == 0, z, chips - 1 - z)
    order = [2 * z for z in range(zn)] + [2 * z + 1 for z in reversed(range(zn))]

    def turn(step):
        return [
            (2 * order[i] + c, 2 * order[(i + step) % chips] + c) for i in range(chips) for c in range(2)
        ]

    right, left = turn(1), turn(-1)
    across = [(i, i ^ 1) for i in range(2 * chips)]

    def send(a, pairs):
        return lax.ppermute(a, "layer", pairs)

    def index(half, i):
        return (core ^ half) * chips + (place + i) % chips

    far = chips // 2
    rounds = [[far]] + [[i, chips - i] for i in range(far - 1, 0, -1)] + [[0]]

    def both(items):
        return jnp.stack([index(h, i) for h in range(2) for i in items]).astype(jnp.int32)

    def scatter_sum(parts, wire, scale, last, ahead=None):
        keeps = [[] for _ in parts]
        others = [[] for _ in parts]

        def compute(r, mark, part=None):
            keep, out = (part or parts[r])(mark)
            keeps[r].append(keep)
            return out

        def swap(r, out, mark=None):
            others[r].append(send(out if mark is None else join(out, mark), across))

        def mine(r, j):
            at = [(k, i) for k, a in enumerate(keeps[r]) for i in range(a.shape[0])][j]
            return (keeps[r][at[0]][at[1]] + others[r][at[0]][at[1]]) * scale

        def corner(message):
            return message[:8, :128].astype(F32)

        swap(0, compute(0, None))
        split = parts[1] if isinstance(parts[1], list) else [parts[1]]
        out = compute(1, keeps[0][0], split[0])
        first = mine(0, 0).astype(wire)
        cut = first.shape[0] // 2
        to_right, to_left = send(first[:cut], right), send(first[cut:], left)
        for r in range(1, far):
            mark = corner(first)
            swap(r, out, mark)
            if r == 1 and len(split) > 1:
                swap(r, compute(r, mark, split[1]))
                mark = keeps[r][1]
            if ahead is not None and r >= 2:
                mark = ahead(r - 2, mark)
            out = compute(r + 1, mark)
            a, b = mine(r, 0), mine(r, 1)
            if r == 1:
                a = jnp.concatenate([a[:cut] + to_right.astype(F32), a[cut:]])
                b = jnp.concatenate([b[:cut], b[cut:] + to_left.astype(F32)])
            else:
                a, b = a + to_right.astype(F32), b + to_left.astype(F32)
            first, second = a.astype(wire), b.astype(wire)
            to_right, to_left = send(first, right), send(second, left)
        mark = corner(first)
        swap(far, out, mark)
        return last(keeps[far][0], others[far][0], to_right, to_left)

    def gather(own, use, lag):
        a, b = send(own, right), send(own, left)
        came = [([(0, 0)], [own])]
        waiting = [([(1, 0)], [send(own, across)])]
        cut = own.shape[0] // 2
        for i in range(1, far):
            if not lag:
                came, waiting = came + waiting, []
            mark = use(sum([c[0] for c in came], []), sum([c[1] for c in came], []))
            came, waiting = waiting, []
            a = join(a, mark)
            places, got = [chips - i, i], [a, b]
            if i < far - 1:
                a, b = send(a, right), send(b, left)
            else:
                a, b = send(a[:cut], right), send(b[cut:], left)
            came.append(([(0, p) for p in places], got))
            waiting.append(([(1, p) for p in places], [send(piece, across) for piece in got]))
        came = came + waiting
        mark = use(sum([c[0] for c in came], []), sum([c[1] for c in came], []))
        last = jnp.concatenate([join(a, mark), b])
        return [(0, far), (1, far)], [last, send(last, across)]

    def where(items):
        return jnp.stack([index(h, i) for h, i in items]).astype(jnp.int32)

    features = basis.shape[0] * 2 * chips
    wire_scale = 2.0 ** math.floor(math.log2(60000.0 / (X_MAX * BASIS_MAX * features)))
    listed = [(h, i) for r in rounds for h in range(2) for i in r]
    x, tiles = start(where(listed), token_ids.reshape(-1, 1), hidden_pool, basis, kb)

    def projected(r):
        first = sum(2 * len(items) for items in rounds[:r])
        return lambda mark: project(first, (len(rounds[r]),) * 2, x, tiles, x if mark is None else mark)

    def rounded(keep, other, to_right, to_left):
        total = (keep[0] + other[0]) * wire_scale + to_right.astype(F32) + to_left.astype(F32)
        return (total * (1.0 / wire_scale)).astype(BF16)

    kept = [far] + rounds[1]
    held = {}

    def ahead(r, mark):
        if r >= len(kept):
            return mark
        held[kept[r]], mark = hold(where([(0, kept[r]), (1, kept[r])]), coeffs, kb, mark)
        return mark

    own = scatter_sum([projected(r) for r in range(far + 1)], F16, wire_scale, rounded, ahead)

    state = {"acc": None, "grad": None}

    def use_forward(items, blocks):
        found = dict(zip(items, blocks))
        near = [item for item in items if item[1] not in held]
        pairs = [i for i in kept if (0, i) in found and (1, i) in found]
        ordered = [found[item] for item in near] + [found[h, i] for i in pairs for h in range(2)]
        assert len(ordered) == len(items)
        state["acc"], mark = predict(where(near), coeffs, ordered, [held[i] for i in pairs], state["acc"])
        if len(held) < len(kept):
            mark = ahead(len(held), mark)
        return mark

    items, last = gather(own, use_forward, True)
    res, low, keep, out = residuals(last, held[far], targets, state["acc"])

    def backed(r):
        return lambda mark: backward(both(rounds[r]), coeffs, low, mark, kb)

    parts = [
        lambda mark: (keep, out),
        [lambda mark, i=i: backward_held([held[i]], low, mark, kb) for i in rounds[1]],
    ]
    parts += [backed(r) for r in range(2, far + 1)]
    own = scatter_sum(parts, BF16, 1.0, finish)
    xt = x.T

    def use_back(items, blocks):
        state["grad"], mark = gradient(where(items), xt, blocks, state["grad"], rank, -1.0 / tok_count)
        return mark

    use_back(*gather(own, use_back, False))
    return res, state["grad"]


def solution(mesh):
    placed = (
        P("groups", None),
        P("groups", "layer"),
        P("layer", "groups"),
        P(None, "groups", "layer"),
        P("groups", None, "layer"),
    )
    count = mesh.shape["layer"]
    body = functools.partial(staged, 4) if count == 16 else plain
    return jax.shard_map(
        body,
        mesh=mesh,
        in_specs=placed,
        out_specs=(P("groups", None, "layer"), P("layer", "groups")),
        check_vma=False,
    )
```

```python
import functools
import math

import jax
import jax.numpy as jnp
from jax import lax
from jax.experimental import pallas as pl
from jax.experimental.pallas import tpu as pltpu
from jax.sharding import PartitionSpec as P

X_MAX = 6.0
BASIS_MAX = 0.046875
F32 = jnp.float32
BF16 = jnp.bfloat16
F16 = jnp.float16
IN_VMEM = pl.BlockSpec(memory_space=pltpu.MemorySpace.VMEM)
IN_SMEM = pl.BlockSpec(memory_space=pltpu.MemorySpace.SMEM)
IN_HBM = pl.BlockSpec(memory_space=pltpu.MemorySpace.HBM)
MIB = 2**20


def params(mib):
    return pltpu.CompilerParams(vmem_limit_bytes=mib * MIB)


def cost(flops, moved):
    return pl.CostEstimate(flops=flops, bytes_accessed=moved, transcendentals=0)


def block(ref, i, size):
    return pl.ds(pl.multiple_of(ref[i] * size, size), size)


def join(value, mark):
    return pl.pallas_call(
        lambda value_ref, mark_ref, out_ref: None,
        out_shape=jax.ShapeDtypeStruct(value.shape, value.dtype),
        in_specs=[IN_VMEM, IN_VMEM],
        out_specs=IN_VMEM,
        input_output_aliases={0: 0},
        compiler_params=params(2),
        name="join",
    )(value, mark)


def start_body(cols, kb, idx_ref, hot_ref, pool_ref, basis_ref, x_ref, tiles_ref, sems):
    n = tiles_ref.shape[0]

    def tile(i):
        return pltpu.make_async_copy(basis_ref.at[:, block(idx_ref, i, kb)], tiles_ref.at[i], sems.at[i])

    for i in range(n):
        tile(i).start()

    @pl.loop(0, x_ref.shape[1] // cols)
    def _(i):
        window = pl.ds(pl.multiple_of(i * cols, cols), cols)
        x_ref[:, window] = jnp.dot(
            hot_ref[...], pool_ref[:, window], preferred_element_type=F32
        ).astype(BF16)

    @pl.loop(0, n)
    def _(i):
        tile(i).wait()


def start(idx, ids, pool, basis, kb):
    rows = ids.shape[0]
    pool_rows, depth = pool.shape
    n = idx.shape[0]
    hot = (ids == lax.broadcasted_iota(jnp.int32, (rows, pool_rows), 1)).astype(BF16)
    return pl.pallas_call(
        functools.partial(start_body, 256, kb),
        out_shape=(
            jax.ShapeDtypeStruct((rows, depth), BF16),
            jax.ShapeDtypeStruct((n, depth, kb), BF16),
        ),
        in_specs=[IN_SMEM, IN_VMEM, IN_VMEM, IN_HBM],
        out_specs=(IN_VMEM, IN_VMEM),
        scratch_shapes=[pltpu.SemaphoreType.DMA((n,))],
        compiler_params=params(36),
        cost_estimate=cost(2 * rows * pool_rows * depth, pool_rows * depth * 2),
        name="start",
    )(idx, hot, pool, basis)


def project_body(first, sizes, x_ref, tiles_ref, mark_ref, *outs):
    base = first
    for out, size in zip(outs, sizes):

        @pl.loop(0, size)
        def _(j, base=base, out=out):
            out[j] = jnp.dot(x_ref[...], tiles_ref[base + j], preferred_element_type=F32)

        base += size


def project(first, sizes, x, tiles, mark):
    rows, depth = x.shape
    kb = tiles.shape[2]
    n = sum(sizes)
    return pl.pallas_call(
        functools.partial(project_body, first, sizes),
        out_shape=tuple(jax.ShapeDtypeStruct((size, rows, kb), F32) for size in sizes),
        in_specs=[IN_VMEM, IN_VMEM, IN_VMEM],
        out_specs=(IN_VMEM,) * len(sizes),
        compiler_params=params(8),
        cost_estimate=cost(2 * n * rows * depth * kb, n * depth * kb * 2),
        name="project",
    )(x, tiles, mark)


def finish(keep, other, to_right, to_left):
    _, kb, rows = keep.shape

    def body(keep_ref, other_ref, right_ref, left_ref, out_ref):
        total = keep_ref[0] + other_ref[0] + right_ref[...].astype(F32) + left_ref[...].astype(F32)
        out_ref[...] = total.T.astype(BF16)

    return pl.pallas_call(
        body,
        out_shape=jax.ShapeDtypeStruct((rows, kb), BF16),
        in_specs=[IN_VMEM] * 4,
        out_specs=IN_VMEM,
        compiler_params=params(8),
        name="finish",
    )(keep, other, to_right, to_left)


def coeff_copy(idx_ref, coeff_ref, buf, sems, kb, l, i):
    return pltpu.make_async_copy(
        coeff_ref.at[l, block(idx_ref, i, kb), :], buf.at[l, pl.ds(i * kb, kb), :], sems.at[l, i]
    )


def start_coeffs(idx_ref, coeff_ref, buf, sems, n, kb):
    @pl.loop(0, buf.shape[0])
    def _(l):
        for i in range(n):
            coeff_copy(idx_ref, coeff_ref, buf, sems, kb, l, i).start()


def wait_coeffs(idx_ref, coeff_ref, buf, sems, n, kb, l):
    for i in range(n):
        coeff_copy(idx_ref, coeff_ref, buf, sems, kb, l, i).wait()


def rows_of(l, size):
    return pl.ds(pl.multiple_of(l * size, size), size)


def wide(pieces, span):
    return jnp.concatenate([piece[span, :] for piece in pieces], axis=1)


def predicted(l, span, pieces, copied, buf, held, held_refs):
    total = None
    if copied:
        total = jnp.dot(wide(pieces[:copied], span), buf[l], preferred_element_type=F32)
    for k in range(held):
        pair = pieces[copied + 2 * k : copied + 2 * k + 2]
        part = jnp.dot(wide(pair, span), held_refs[k][l], preferred_element_type=F32)
        total = part if total is None else total + part
    return total


def predict_body(n, held, first, idx_ref, coeff_ref, *refs):
    count = n + 2 * held
    pieces, held_refs, rest = refs[:count], refs[count : count + held], refs[count + held :]
    if first:
        out_ref, mark_ref, buf, sems = rest
    else:
        acc_ref, out_ref, mark_ref, buf, sems = rest
    layer_count = buf.shape[0]
    mark_ref[...] = jnp.zeros_like(mark_ref)
    rows, kb = pieces[0].shape
    toks = rows // layer_count
    start_coeffs(idx_ref, coeff_ref, buf, sems, n, kb)

    @pl.loop(0, layer_count)
    def _(l):
        span = rows_of(l, toks)
        wait_coeffs(idx_ref, coeff_ref, buf, sems, n, kb, l)
        part = predicted(l, span, pieces, n, buf, held, held_refs)
        out_ref[span, :] = part if first else acc_ref[span, :] + part


def coeff_scratch(coeffs, n, kb):
    layer_count, _, width = coeffs.shape
    return [pltpu.VMEM((layer_count, n * kb, width), BF16), pltpu.SemaphoreType.DMA((layer_count, n))]


def predict(idx, coeffs, pieces, tiles, acc):
    n = idx.shape[0]
    held = len(tiles)
    rows, kb = pieces[0].shape
    layer_count, _, width = coeffs.shape
    first = acc is None
    inputs = len(pieces) + held
    return pl.pallas_call(
        functools.partial(predict_body, n, held, first),
        out_shape=(jax.ShapeDtypeStruct((rows, width), F32), jax.ShapeDtypeStruct((8, 128), F32)),
        in_specs=[IN_SMEM, IN_HBM] + [IN_VMEM] * (inputs + (not first)),
        out_specs=(IN_VMEM, IN_VMEM),
        input_output_aliases={} if first else {inputs + 2: 0},
        scratch_shapes=coeff_scratch(coeffs, n, kb),
        compiler_params=params(4 * n + 3),
        cost_estimate=cost(8 * len(pieces) * rows * kb * width, layer_count * n * kb * width * 2),
        name="predict",
    )(idx, coeffs, *pieces, *tiles, *([] if first else [acc]))


def hold_body(n, kb, idx_ref, coeff_ref, after_ref, tiles_ref, mark_ref, sems):
    mark_ref[...] = jnp.zeros_like(mark_ref)
    start_coeffs(idx_ref, coeff_ref, tiles_ref, sems, n, kb)

    @pl.loop(0, tiles_ref.shape[0])
    def _(l):
        wait_coeffs(idx_ref, coeff_ref, tiles_ref, sems, n, kb, l)


def hold(idx, coeffs, kb, mark):
    n = idx.shape[0]
    layer_count, _, width = coeffs.shape
    return pl.pallas_call(
        functools.partial(hold_body, n, kb),
        out_shape=(
            jax.ShapeDtypeStruct((layer_count, n * kb, width), BF16),
            jax.ShapeDtypeStruct((8, 128), F32),
        ),
        in_specs=[IN_SMEM, IN_HBM, IN_VMEM],
        out_specs=(IN_VMEM, IN_VMEM),
        scratch_shapes=coeff_scratch(coeffs, n, kb)[1:],
        compiler_params=params(12),
        cost_estimate=cost(0, layer_count * n * kb * width * 2),
        name="hold",
    )(idx, coeffs, mark)


def back_blocks(low, tiles, l, outs, toks):
    kb = outs[0].shape[0]
    parts = [
        lax.dot_general(
            tiles[l + j],
            low[j * toks : (j + 1) * toks, :],
            (((1,), (1,)), ((), ())),
            preferred_element_type=F32,
        )
        for j in range(2)
    ]
    both = jnp.concatenate(parts, axis=1)
    lanes = pl.ds(pl.multiple_of(l * toks, 2 * toks), 2 * toks)
    for i, out in enumerate(outs):
        out[:, lanes] = both[i * kb : (i + 1) * kb, :]


def residual_body(a_ref, b_ref, tiles_ref, target_ref, acc_ref, res_ref, low_ref, keep_ref, send_ref):
    layer_count, toks, _ = target_ref.shape

    @pl.loop(0, layer_count, step=2)
    def _(l):
        spans = [rows_of(l + j, toks) for j in range(2)]
        parts = [predicted(l + j, spans[j], (a_ref, b_ref), 0, None, 1, (tiles_ref,)) for j in range(2)]
        lows = []
        for j, (span, part) in enumerate(zip(spans, parts)):
            res = target_ref[l + j].astype(F32) - (acc_ref[span, :] + part)
            res_ref[l + j] = res
            lows.append(res.astype(BF16))
            low_ref[span, :] = lows[j]
        low = jnp.concatenate(lows, axis=0)
        back_blocks(low, tiles_ref, l, [keep_ref.at[0], send_ref.at[0]], toks)


def residuals(pieces, tiles, targets, acc):
    rows, kb = pieces[0].shape
    layer_count, _, width = targets.shape
    half = jax.ShapeDtypeStruct((1, kb, rows), F32)
    return pl.pallas_call(
        residual_body,
        out_shape=(
            jax.ShapeDtypeStruct(targets.shape, F32),
            jax.ShapeDtypeStruct((rows, width), BF16),
            half,
            half,
        ),
        in_specs=[IN_VMEM] * 5,
        out_specs=(IN_VMEM,) * 4,
        compiler_params=params(8),
        cost_estimate=cost(32 * rows * kb * width, tiles.size * 2),
        name="residuals",
    )(*pieces, tiles, targets, acc)


def backward_body(n, idx_ref, coeff_ref, low_ref, mark_ref, keep_ref, send_ref, buf, sems):
    layer_count = buf.shape[0]
    m, kb, _ = keep_ref.shape
    toks = low_ref.shape[0] // layer_count
    start_coeffs(idx_ref, coeff_ref, buf, sems, n, kb)

    @pl.loop(0, layer_count, step=2)
    def _(l):
        for j in range(2):
            wait_coeffs(idx_ref, coeff_ref, buf, sems, n, kb, l + j)
        pair = pl.ds(pl.multiple_of(l * toks, 2 * toks), 2 * toks)
        outs = [keep_ref.at[i] for i in range(m)] + [send_ref.at[i] for i in range(m)]
        back_blocks(low_ref[pair, :], buf, l, outs, toks)


def backward(idx, coeffs, low, mark, kb):
    n = idx.shape[0]
    rows = low.shape[0]
    layer_count, _, width = coeffs.shape
    half = jax.ShapeDtypeStruct((n // 2, kb, rows), F32)
    return pl.pallas_call(
        functools.partial(backward_body, n),
        out_shape=(half, half),
        in_specs=[IN_SMEM, IN_HBM, IN_VMEM, IN_VMEM],
        out_specs=(IN_VMEM,) * 2,
        scratch_shapes=coeff_scratch(coeffs, n, kb),
        compiler_params=params(4 * n + 3),
        cost_estimate=cost(8 * n * rows * kb * width, layer_count * n * kb * width * 2),
        name="backward",
    )(idx, coeffs, low, mark)


def backward_held_body(layer_count, low_ref, mark_ref, *refs):
    tiles, (keep_ref, send_ref) = refs[:-2], refs[-2:]
    toks = low_ref.shape[0] // layer_count

    @pl.loop(0, layer_count, step=4)
    def _(first):
        for j in range(0, 4, 2):
            l = first + j
            pair = pl.ds(pl.multiple_of(l * toks, 2 * toks), 2 * toks)
            for i, tile in enumerate(tiles):
                back_blocks(low_ref[pair, :], tile, l, [keep_ref.at[i], send_ref.at[i]], toks)


def backward_held(tiles, low, mark, kb):
    m = len(tiles)
    rows = low.shape[0]
    layer_count, _, width = tiles[0].shape
    half = jax.ShapeDtypeStruct((m, kb, rows), F32)
    return pl.pallas_call(
        functools.partial(backward_held_body, layer_count),
        out_shape=(half, half),
        in_specs=[IN_VMEM] * (m + 2),
        out_specs=(IN_VMEM,) * 2,
        compiler_params=params(8),
        cost_estimate=cost(16 * m * rows * kb * width, m * tiles[0].size * 2),
        name="backward_held",
    )(low, mark, *tiles)


def gradient_body(n, scale, first, idx_ref, xt_ref, *refs):
    pieces, (out_ref, mark_ref, buf, sems) = refs[:n], refs[n + (not first) :]
    mark_ref[...] = jnp.zeros_like(mark_ref)
    kb = buf.shape[2]
    depth = buf.shape[1]
    copies = []
    for i in range(n):

        @pl.loop(0, 2)
        def _(r, i=i):
            span = rows_of(r, depth // 2)
            buf[i, span, :] = jnp.dot(xt_ref[span, :], pieces[i][...], preferred_element_type=F32) * scale

        copies.append(
            pltpu.make_async_copy(buf.at[i], out_ref.at[:, block(idx_ref, i, kb)], sems.at[i])
        )
        copies[-1].start()
    for copy in copies:
        copy.wait()


def gradient(idx, xt, pieces, grad, width, scale):
    n = len(pieces)
    kb = pieces[0].shape[1]
    depth, rows = xt.shape
    first = grad is None
    return pl.pallas_call(
        functools.partial(gradient_body, n, scale, first),
        out_shape=(jax.ShapeDtypeStruct((depth, width), F32), jax.ShapeDtypeStruct((8, 128), F32)),
        in_specs=[IN_SMEM] + [IN_VMEM] * (n + 1) + [IN_HBM] * (not first),
        out_specs=(IN_HBM, IN_VMEM),
        input_output_aliases={} if first else {n + 2: 0},
        scratch_shapes=[pltpu.VMEM((n, depth, kb), F32), pltpu.SemaphoreType.DMA((n,))],
        compiler_params=params(16),
        cost_estimate=cost(2 * n * depth * rows * kb, n * depth * kb * 4),
        name="gradient",
    )(idx, xt, *pieces, *([] if first else [grad]))


def plain(token_ids, hidden_pool, basis, coeffs, targets):
    layer_count, tok_count = token_ids.shape
    x_local = jnp.take(hidden_pool, token_ids.reshape(-1), axis=0)
    share = lax.psum_scatter(
        lax.dot_general(basis, x_local, (((0,), (1,)), ((), ())), preferred_element_type=F32),
        "layer",
        scatter_dimension=0,
        tiled=True,
    ).astype(BF16)
    piece = lax.all_gather(share, "layer", axis=0, tiled=True)
    shaped = piece.reshape(piece.shape[0], layer_count, tok_count)
    predicted = jnp.einsum("kls,lko->lso", shaped, coeffs, preferred_element_type=F32)
    residual = targets.astype(F32) - predicted
    summed = jnp.einsum("lko,lso->kls", coeffs, residual.astype(BF16), preferred_element_type=F32)
    summed = summed.reshape(basis.shape[1], -1)
    back = lax.psum_scatter(summed, "layer", scatter_dimension=0, tiled=True).astype(BF16)
    back = lax.all_gather(back, "layer", axis=0, tiled=True)
    product = lax.dot_general(x_local, back, (((0,), (1,)), ((), ())), preferred_element_type=F32)
    return residual, product * (-1.0 / tok_count)


def staged(zn, token_ids, hidden_pool, basis, coeffs, targets):
    chips = 2 * zn
    tok_count = token_ids.shape[1]
    rank = basis.shape[1]
    kb = rank // (2 * chips)
    me = lax.axis_index("layer")
    core, y, z = me % 2, (me // 2) % 2, me // 4
    place = jnp.where(y == 0, z, chips - 1 - z)
    order = [2 * z for z in range(zn)] + [2 * z + 1 for z in reversed(range(zn))]

    def turn(step):
        return [
            (2 * order[i] + c, 2 * order[(i + step) % chips] + c) for i in range(chips) for c in range(2)
        ]

    right, left = turn(1), turn(-1)
    across = [(i, i ^ 1) for i in range(2 * chips)]

    def send(a, pairs):
        return lax.ppermute(a, "layer", pairs)

    def index(half, i):
        return (core ^ half) * chips + (place + i) % chips

    far = chips // 2
    rounds = [[far]] + [[i, chips - i] for i in range(far - 1, 0, -1)] + [[0]]

    def both(items):
        return jnp.stack([index(h, i) for h in range(2) for i in items]).astype(jnp.int32)

    def scatter_sum(parts, wire, scale, last, ahead=None):
        keeps = [[] for _ in parts]
        others = [[] for _ in parts]

        def compute(r, mark, part=None):
            keep, out = (part or parts[r])(mark)
            keeps[r].append(keep)
            return out

        def swap(r, out, mark=None):
            others[r].append(send(out if mark is None else join(out, mark), across))

        def mine(r, j):
            at = [(k, i) for k, a in enumerate(keeps[r]) for i in range(a.shape[0])][j]
            return (keeps[r][at[0]][at[1]] + others[r][at[0]][at[1]]) * scale

        def corner(message):
            return message[:8, :128].astype(F32)

        swap(0, compute(0, None))
        split = parts[1] if isinstance(parts[1], list) else [parts[1]]
        out = compute(1, keeps[0][0], split[0])
        first = mine(0, 0).astype(wire)
        cut = first.shape[0] // 2
        to_right, to_left = send(first[:cut], right), send(first[cut:], left)
        for r in range(1, far):
            mark = corner(first)
            swap(r, out, mark)
            if r == 1 and len(split) > 1:
                swap(r, compute(r, mark, split[1]))
                mark = keeps[r][1]
            if ahead is not None and r >= 2:
                mark = ahead(r - 2, mark)
            out = compute(r + 1, mark)
            a, b = mine(r, 0), mine(r, 1)
            if r == 1:
                a = jnp.concatenate([a[:cut] + to_right.astype(F32), a[cut:]])
                b = jnp.concatenate([b[:cut], b[cut:] + to_left.astype(F32)])
            else:
                a, b = a + to_right.astype(F32), b + to_left.astype(F32)
            first, second = a.astype(wire), b.astype(wire)
            to_right, to_left = send(first, right), send(second, left)
        mark = corner(first)
        swap(far, out, mark)
        return last(keeps[far][0], others[far][0], to_right, to_left)

    def gather(own, use, lag):
        a, b = send(own, right), send(own, left)
        came = [([(0, 0)], [own])]
        waiting = [([(1, 0)], [send(own, across)])]
        cut = own.shape[0] // 2
        for i in range(1, far):
            if not lag:
                came, waiting = came + waiting, []
            mark = use(sum([c[0] for c in came], []), sum([c[1] for c in came], []))
            came, waiting = waiting, []
            a = join(a, mark)
            places, got = [chips - i, i], [a, b]
            if i < far - 1:
                a, b = send(a, right), send(b, left)
            else:
                a, b = send(a[:cut], right), send(b[cut:], left)
            came.append(([(0, p) for p in places], got))
            waiting.append(([(1, p) for p in places], [send(piece, across) for piece in got]))
        came = came + waiting
        mark = use(sum([c[0] for c in came], []), sum([c[1] for c in came], []))
        last = jnp.concatenate([join(a, mark), b])
        return [(0, far), (1, far)], [last, send(last, across)]

    def where(items):
        return jnp.stack([index(h, i) for h, i in items]).astype(jnp.int32)

    features = basis.shape[0] * 2 * chips
    wire_scale = 2.0 ** math.floor(math.log2(60000.0 / (X_MAX * BASIS_MAX * features)))
    listed = [(h, i) for r in rounds for h in range(2) for i in r]
    x, tiles = start(where(listed), token_ids.reshape(-1, 1), hidden_pool, basis, kb)

    def projected(r):
        first = sum(2 * len(items) for items in rounds[:r])
        return lambda mark: project(first, (len(rounds[r]),) * 2, x, tiles, x if mark is None else mark)

    def rounded(keep, other, to_right, to_left):
        total = (keep[0] + other[0]) * wire_scale + to_right.astype(F32) + to_left.astype(F32)
        return (total * (1.0 / wire_scale)).astype(BF16)

    kept = [far] + rounds[1]
    held = {}

    def ahead(r, mark):
        if r >= len(kept):
            return mark
        held[kept[r]], mark = hold(where([(0, kept[r]), (1, kept[r])]), coeffs, kb, mark)
        return mark

    own = scatter_sum([projected(r) for r in range(far + 1)], F16, wire_scale, rounded, ahead)

    state = {"acc": None, "grad": None}

    def use_forward(items, blocks):
        found = dict(zip(items, blocks))
        near = [item for item in items if item[1] not in held]
        pairs = [i for i in kept if (0, i) in found and (1, i) in found]
        ordered = [found[item] for item in near] + [found[h, i] for i in pairs for h in range(2)]
        assert len(ordered) == len(items)
        state["acc"], mark = predict(where(near), coeffs, ordered, [held[i] for i in pairs], state["acc"])
        if len(held) < len(kept):
            mark = ahead(len(held), mark)
        return mark

    items, last = gather(own, use_forward, True)
    res, low, keep, out = residuals(last, held[far], targets, state["acc"])

    def backed(r):
        return lambda mark: backward(both(rounds[r]), coeffs, low, mark, kb)

    parts = [
        lambda mark: (keep, out),
        [lambda mark, i=i: backward_held([held[i]], low, mark, kb) for i in rounds[1]],
    ]
    parts += [backed(r) for r in range(2, far + 1)]
    own = scatter_sum(parts, BF16, 1.0, finish)
    xt = x.T

    def use_back(items, blocks):
        state["grad"], mark = gradient(where(items), xt, blocks, state["grad"], rank, -1.0 / tok_count)
        return mark

    use_back(*gather(own, use_back, False))
    return res, state["grad"]


def solution(mesh):
    placed = (
        P("groups", None),
        P("groups", "layer"),
        P("layer", "groups"),
        P(None, "groups", "layer"),
        P("groups", None, "layer"),
    )
    count = mesh.shape["layer"]
    body = functools.partial(staged, 4) if count == 16 else plain
    return jax.shard_map(
        body,
        mesh=mesh,
        in_specs=placed,
        out_specs=(P("groups", None, "layer"), P("layer", "groups")),
        check_vma=False,
    )
```

```python
import functools
import math

import jax
import jax.numpy as jnp
from jax import lax
from jax.experimental import pallas as pl
from jax.experimental.pallas import tpu as pltpu
from jax.sharding import PartitionSpec as P

X_MAX = 6.0
BASIS_MAX = 0.046875
F32 = jnp.float32
BF16 = jnp.bfloat16
F16 = jnp.float16
IN_VMEM = pl.BlockSpec(memory_space=pltpu.MemorySpace.VMEM)
IN_SMEM = pl.BlockSpec(memory_space=pltpu.MemorySpace.SMEM)
IN_HBM = pl.BlockSpec(memory_space=pltpu.MemorySpace.HBM)
MIB = 2**20


def params(mib):
    return pltpu.CompilerParams(vmem_limit_bytes=mib * MIB)


def cost(flops, moved):
    return pl.CostEstimate(flops=flops, bytes_accessed=moved, transcendentals=0)


def block(ref, i, size):
    return pl.ds(pl.multiple_of(ref[i] * size, size), size)


def join(value, mark):
    return pl.pallas_call(
        lambda value_ref, mark_ref, out_ref: None,
        out_shape=jax.ShapeDtypeStruct(value.shape, value.dtype),
        in_specs=[IN_VMEM, IN_VMEM],
        out_specs=IN_VMEM,
        input_output_aliases={0: 0},
        compiler_params=params(2),
        name="join",
    )(value, mark)


def start_body(cols, kb, idx_ref, hot_ref, pool_ref, basis_ref, x_ref, tiles_ref, sems):
    n = tiles_ref.shape[0]

    def tile(i):
        return pltpu.make_async_copy(basis_ref.at[:, block(idx_ref, i, kb)], tiles_ref.at[i], sems.at[i])

    for i in range(n):
        tile(i).start()

    @pl.loop(0, x_ref.shape[1] // cols)
    def _(i):
        window = pl.ds(pl.multiple_of(i * cols, cols), cols)
        x_ref[:, window] = jnp.dot(
            hot_ref[...], pool_ref[:, window], preferred_element_type=F32
        ).astype(BF16)

    @pl.loop(0, n)
    def _(i):
        tile(i).wait()


def start(idx, ids, pool, basis, kb):
    rows = ids.shape[0]
    pool_rows, depth = pool.shape
    n = idx.shape[0]
    hot = (ids == lax.broadcasted_iota(jnp.int32, (rows, pool_rows), 1)).astype(BF16)
    return pl.pallas_call(
        functools.partial(start_body, 256, kb),
        out_shape=(
            jax.ShapeDtypeStruct((rows, depth), BF16),
            jax.ShapeDtypeStruct((n, depth, kb), BF16),
        ),
        in_specs=[IN_SMEM, IN_VMEM, IN_VMEM, IN_HBM],
        out_specs=(IN_VMEM, IN_VMEM),
        scratch_shapes=[pltpu.SemaphoreType.DMA((n,))],
        compiler_params=params(36),
        cost_estimate=cost(2 * rows * pool_rows * depth, pool_rows * depth * 2),
        name="start",
    )(idx, hot, pool, basis)


def project_body(first, sizes, x_ref, tiles_ref, mark_ref, *outs):
    base = first
    for out, size in zip(outs, sizes):

        @pl.loop(0, size)
        def _(j, base=base, out=out):
            out[j] = jnp.dot(x_ref[...], tiles_ref[base + j], preferred_element_type=F32)

        base += size


def project(first, sizes, x, tiles, mark):
    rows, depth = x.shape
    kb = tiles.shape[2]
    n = sum(sizes)
    return pl.pallas_call(
        functools.partial(project_body, first, sizes),
        out_shape=tuple(jax.ShapeDtypeStruct((size, rows, kb), F32) for size in sizes),
        in_specs=[IN_VMEM, IN_VMEM, IN_VMEM],
        out_specs=(IN_VMEM,) * len(sizes),
        compiler_params=params(8),
        cost_estimate=cost(2 * n * rows * depth * kb, n * depth * kb * 2),
        name="project",
    )(x, tiles, mark)


def finish(keep, other, to_right, to_left):
    _, kb, rows = keep.shape

    def body(keep_ref, other_ref, right_ref, left_ref, out_ref):
        total = keep_ref[0] + other_ref[0] + right_ref[...].astype(F32) + left_ref[...].astype(F32)
        out_ref[...] = total.T.astype(BF16)

    return pl.pallas_call(
        body,
        out_shape=jax.ShapeDtypeStruct((rows, kb), BF16),
        in_specs=[IN_VMEM] * 4,
        out_specs=IN_VMEM,
        compiler_params=params(8),
        name="finish",
    )(keep, other, to_right, to_left)


def coeff_copy(idx_ref, coeff_ref, buf, sems, kb, l, i):
    return pltpu.make_async_copy(
        coeff_ref.at[l, block(idx_ref, i, kb), :], buf.at[l, pl.ds(i * kb, kb), :], sems.at[l, i]
    )


def start_coeffs(idx_ref, coeff_ref, buf, sems, n, kb):
    @pl.loop(0, buf.shape[0])
    def _(l):
        for i in range(n):
            coeff_copy(idx_ref, coeff_ref, buf, sems, kb, l, i).start()


def wait_coeffs(idx_ref, coeff_ref, buf, sems, n, kb, l):
    for i in range(n):
        coeff_copy(idx_ref, coeff_ref, buf, sems, kb, l, i).wait()


def rows_of(l, size):
    return pl.ds(pl.multiple_of(l * size, size), size)


def wide(pieces, span):
    return jnp.concatenate([piece[span, :] for piece in pieces], axis=1)


def predicted(l, span, pieces, copied, buf, held, held_refs):
    total = None
    if copied:
        total = jnp.dot(wide(pieces[:copied], span), buf[l], preferred_element_type=F32)
    for k in range(held):
        pair = pieces[copied + 2 * k : copied + 2 * k + 2]
        part = jnp.dot(wide(pair, span), held_refs[k][l], preferred_element_type=F32)
        total = part if total is None else total + part
    return total


def predict_body(n, held, first, idx_ref, coeff_ref, *refs):
    count = n + 2 * held
    pieces, held_refs, rest = refs[:count], refs[count : count + held], refs[count + held :]
    if first:
        out_ref, mark_ref, buf, sems = rest
    else:
        acc_ref, out_ref, mark_ref, buf, sems = rest
    layer_count = buf.shape[0]
    mark_ref[...] = jnp.zeros_like(mark_ref)
    rows, kb = pieces[0].shape
    toks = rows // layer_count
    start_coeffs(idx_ref, coeff_ref, buf, sems, n, kb)

    @pl.loop(0, layer_count)
    def _(l):
        span = rows_of(l, toks)
        wait_coeffs(idx_ref, coeff_ref, buf, sems, n, kb, l)
        part = predicted(l, span, pieces, n, buf, held, held_refs)
        out_ref[span, :] = part if first else acc_ref[span, :] + part


def coeff_scratch(coeffs, n, kb):
    layer_count, _, width = coeffs.shape
    return [pltpu.VMEM((layer_count, n * kb, width), BF16), pltpu.SemaphoreType.DMA((layer_count, n))]


def predict(idx, coeffs, pieces, tiles, acc):
    n = idx.shape[0]
    held = len(tiles)
    rows, kb = pieces[0].shape
    layer_count, _, width = coeffs.shape
    first = acc is None
    inputs = len(pieces) + held
    return pl.pallas_call(
        functools.partial(predict_body, n, held, first),
        out_shape=(jax.ShapeDtypeStruct((rows, width), F32), jax.ShapeDtypeStruct((8, 128), F32)),
        in_specs=[IN_SMEM, IN_HBM] + [IN_VMEM] * (inputs + (not first)),
        out_specs=(IN_VMEM, IN_VMEM),
        input_output_aliases={} if first else {inputs + 2: 0},
        scratch_shapes=coeff_scratch(coeffs, n, kb),
        compiler_params=params(4 * n + 3),
        cost_estimate=cost(8 * len(pieces) * rows * kb * width, layer_count * n * kb * width * 2),
        name="predict",
    )(idx, coeffs, *pieces, *tiles, *([] if first else [acc]))


def hold_body(n, kb, idx_ref, coeff_ref, after_ref, tiles_ref, mark_ref, sems):
    mark_ref[...] = jnp.zeros_like(mark_ref)
    start_coeffs(idx_ref, coeff_ref, tiles_ref, sems, n, kb)

    @pl.loop(0, tiles_ref.shape[0])
    def _(l):
        wait_coeffs(idx_ref, coeff_ref, tiles_ref, sems, n, kb, l)


def hold(idx, coeffs, kb, mark):
    n = idx.shape[0]
    layer_count, _, width = coeffs.shape
    return pl.pallas_call(
        functools.partial(hold_body, n, kb),
        out_shape=(
            jax.ShapeDtypeStruct((layer_count, n * kb, width), BF16),
            jax.ShapeDtypeStruct((8, 128), F32),
        ),
        in_specs=[IN_SMEM, IN_HBM, IN_VMEM],
        out_specs=(IN_VMEM, IN_VMEM),
        scratch_shapes=coeff_scratch(coeffs, n, kb)[1:],
        compiler_params=params(12),
        cost_estimate=cost(0, layer_count * n * kb * width * 2),
        name="hold",
    )(idx, coeffs, mark)


def back_blocks(low, tiles, l, outs, toks):
    kb = outs[0].shape[0]
    parts = [
        lax.dot_general(
            tiles[l + j],
            low[j * toks : (j + 1) * toks, :],
            (((1,), (1,)), ((), ())),
            preferred_element_type=F32,
        )
        for j in range(2)
    ]
    both = jnp.concatenate(parts, axis=1)
    lanes = pl.ds(pl.multiple_of(l * toks, 2 * toks), 2 * toks)
    for i, out in enumerate(outs):
        out[:, lanes] = both[i * kb : (i + 1) * kb, :]


def residual_body(a_ref, b_ref, tiles_ref, target_ref, acc_ref, res_ref, low_ref, keep_ref, send_ref):
    layer_count, toks, _ = target_ref.shape

    @pl.loop(0, layer_count, step=2)
    def _(l):
        spans = [rows_of(l + j, toks) for j in range(2)]
        parts = [predicted(l + j, spans[j], (a_ref, b_ref), 0, None, 1, (tiles_ref,)) for j in range(2)]
        lows = []
        for j, (span, part) in enumerate(zip(spans, parts)):
            res = target_ref[l + j].astype(F32) - (acc_ref[span, :] + part)
            res_ref[l + j] = res
            lows.append(res.astype(BF16))
            low_ref[span, :] = lows[j]
        low = jnp.concatenate(lows, axis=0)
        back_blocks(low, tiles_ref, l, [keep_ref.at[0], send_ref.at[0]], toks)


def residuals(pieces, tiles, targets, acc):
    rows, kb = pieces[0].shape
    layer_count, _, width = targets.shape
    half = jax.ShapeDtypeStruct((1, kb, rows), F32)
    return pl.pallas_call(
        residual_body,
        out_shape=(
            jax.ShapeDtypeStruct(targets.shape, F32),
            jax.ShapeDtypeStruct((rows, width), BF16),
            half,
            half,
        ),
        in_specs=[IN_VMEM] * 5,
        out_specs=(IN_VMEM,) * 4,
        compiler_params=params(8),
        cost_estimate=cost(32 * rows * kb * width, tiles.size * 2),
        name="residuals",
    )(*pieces, tiles, targets, acc)


def backward_body(n, idx_ref, coeff_ref, low_ref, mark_ref, keep_ref, send_ref, buf, sems):
    layer_count = buf.shape[0]
    m, kb, _ = keep_ref.shape
    toks = low_ref.shape[0] // layer_count
    start_coeffs(idx_ref, coeff_ref, buf, sems, n, kb)

    @pl.loop(0, layer_count, step=2)
    def _(l):
        for j in range(2):
            wait_coeffs(idx_ref, coeff_ref, buf, sems, n, kb, l + j)
        pair = pl.ds(pl.multiple_of(l * toks, 2 * toks), 2 * toks)
        outs = [keep_ref.at[i] for i in range(m)] + [send_ref.at[i] for i in range(m)]
        back_blocks(low_ref[pair, :], buf, l, outs, toks)


def backward(idx, coeffs, low, mark, kb):
    n = idx.shape[0]
    rows = low.shape[0]
    layer_count, _, width = coeffs.shape
    half = jax.ShapeDtypeStruct((n // 2, kb, rows), F32)
    return pl.pallas_call(
        functools.partial(backward_body, n),
        out_shape=(half, half),
        in_specs=[IN_SMEM, IN_HBM, IN_VMEM, IN_VMEM],
        out_specs=(IN_VMEM,) * 2,
        scratch_shapes=coeff_scratch(coeffs, n, kb),
        compiler_params=params(4 * n + 3),
        cost_estimate=cost(8 * n * rows * kb * width, layer_count * n * kb * width * 2),
        name="backward",
    )(idx, coeffs, low, mark)


def backward_held_body(layer_count, low_ref, mark_ref, *refs):
    tiles, (keep_ref, send_ref) = refs[:-2], refs[-2:]
    toks = low_ref.shape[0] // layer_count

    @pl.loop(0, layer_count, step=4)
    def _(first):
        for j in range(0, 4, 2):
            l = first + j
            pair = pl.ds(pl.multiple_of(l * toks, 2 * toks), 2 * toks)
            for i, tile in enumerate(tiles):
                back_blocks(low_ref[pair, :], tile, l, [keep_ref.at[i], send_ref.at[i]], toks)


def backward_held(tiles, low, mark, kb):
    m = len(tiles)
    rows = low.shape[0]
    layer_count, _, width = tiles[0].shape
    half = jax.ShapeDtypeStruct((m, kb, rows), F32)
    return pl.pallas_call(
        functools.partial(backward_held_body, layer_count),
        out_shape=(half, half),
        in_specs=[IN_VMEM] * (m + 2),
        out_specs=(IN_VMEM,) * 2,
        compiler_params=params(8),
        cost_estimate=cost(16 * m * rows * kb * width, m * tiles[0].size * 2),
        name="backward_held",
    )(low, mark, *tiles)


def gradient_body(n, scale, first, idx_ref, xt_ref, *refs):
    pieces, (out_ref, mark_ref, buf, sems) = refs[:n], refs[n + (not first) :]
    mark_ref[...] = jnp.zeros_like(mark_ref)
    kb = buf.shape[2]
    depth = buf.shape[1]
    copies = []
    for i in range(n):
        for r in range(2):
            span = slice(r * depth // 2, (r + 1) * depth // 2)
            buf[i, span, :] = jnp.dot(xt_ref[span, :], pieces[i][...], preferred_element_type=F32) * scale
            copies.append(
                pltpu.make_async_copy(
                    buf.at[i, span, :], out_ref.at[span, block(idx_ref, i, kb)], sems.at[i, r]
                )
            )
            copies[-1].start()
    for copy in copies:
        copy.wait()


def gradient(idx, xt, pieces, grad, width, scale):
    n = len(pieces)
    kb = pieces[0].shape[1]
    depth, rows = xt.shape
    first = grad is None
    return pl.pallas_call(
        functools.partial(gradient_body, n, scale, first),
        out_shape=(jax.ShapeDtypeStruct((depth, width), F32), jax.ShapeDtypeStruct((8, 128), F32)),
        in_specs=[IN_SMEM] + [IN_VMEM] * (n + 1) + [IN_HBM] * (not first),
        out_specs=(IN_HBM, IN_VMEM),
        input_output_aliases={} if first else {n + 2: 0},
        scratch_shapes=[pltpu.VMEM((n, depth, kb), F32), pltpu.SemaphoreType.DMA((n, 2))],
        compiler_params=params(16),
        cost_estimate=cost(2 * n * depth * rows * kb, n * depth * kb * 4),
        name="gradient",
    )(idx, xt, *pieces, *([] if first else [grad]))


def plain(token_ids, hidden_pool, basis, coeffs, targets):
    layer_count, tok_count = token_ids.shape
    x_local = jnp.take(hidden_pool, token_ids.reshape(-1), axis=0)
    share = lax.psum_scatter(
        lax.dot_general(basis, x_local, (((0,), (1,)), ((), ())), preferred_element_type=F32),
        "layer",
        scatter_dimension=0,
        tiled=True,
    ).astype(BF16)
    piece = lax.all_gather(share, "layer", axis=0, tiled=True)
    shaped = piece.reshape(piece.shape[0], layer_count, tok_count)
    predicted = jnp.einsum("kls,lko->lso", shaped, coeffs, preferred_element_type=F32)
    residual = targets.astype(F32) - predicted
    summed = jnp.einsum("lko,lso->kls", coeffs, residual.astype(BF16), preferred_element_type=F32)
    summed = summed.reshape(basis.shape[1], -1)
    back = lax.psum_scatter(summed, "layer", scatter_dimension=0, tiled=True).astype(BF16)
    back = lax.all_gather(back, "layer", axis=0, tiled=True)
    product = lax.dot_general(x_local, back, (((0,), (1,)), ((), ())), preferred_element_type=F32)
    return residual, product * (-1.0 / tok_count)


def staged(zn, token_ids, hidden_pool, basis, coeffs, targets):
    chips = 2 * zn
    tok_count = token_ids.shape[1]
    rank = basis.shape[1]
    kb = rank // (2 * chips)
    me = lax.axis_index("layer")
    core, y, z = me % 2, (me // 2) % 2, me // 4
    place = jnp.where(y == 0, z, chips - 1 - z)
    order = [2 * z for z in range(zn)] + [2 * z + 1 for z in reversed(range(zn))]

    def turn(step):
        return [
            (2 * order[i] + c, 2 * order[(i + step) % chips] + c) for i in range(chips) for c in range(2)
        ]

    right, left = turn(1), turn(-1)
    across = [(i, i ^ 1) for i in range(2 * chips)]

    def send(a, pairs):
        return lax.ppermute(a, "layer", pairs)

    def index(half, i):
        return (core ^ half) * chips + (place + i) % chips

    far = chips // 2
    rounds = [[far]] + [[i, chips - i] for i in range(far - 1, 0, -1)] + [[0]]

    def both(items):
        return jnp.stack([index(h, i) for h in range(2) for i in items]).astype(jnp.int32)

    def scatter_sum(parts, wire, scale, last, ahead=None):
        keeps = [[] for _ in parts]
        others = [[] for _ in parts]

        def compute(r, mark, part=None):
            keep, out = (part or parts[r])(mark)
            keeps[r].append(keep)
            return out

        def swap(r, out, mark=None):
            others[r].append(send(out if mark is None else join(out, mark), across))

        def mine(r, j):
            at = [(k, i) for k, a in enumerate(keeps[r]) for i in range(a.shape[0])][j]
            return (keeps[r][at[0]][at[1]] + others[r][at[0]][at[1]]) * scale

        def corner(message):
            return message[:8, :128].astype(F32)

        swap(0, compute(0, None))
        split = parts[1] if isinstance(parts[1], list) else [parts[1]]
        out = compute(1, keeps[0][0], split[0])
        first = mine(0, 0).astype(wire)
        cut = first.shape[0] // 2
        to_right, to_left = send(first[:cut], right), send(first[cut:], left)
        for r in range(1, far):
            mark = corner(first)
            swap(r, out, mark)
            if r == 1 and len(split) > 1:
                swap(r, compute(r, mark, split[1]))
                mark = keeps[r][1]
            if ahead is not None and r >= 2:
                mark = ahead(r - 2, mark)
            out = compute(r + 1, mark)
            a, b = mine(r, 0), mine(r, 1)
            if r == 1:
                a = jnp.concatenate([a[:cut] + to_right.astype(F32), a[cut:]])
                b = jnp.concatenate([b[:cut], b[cut:] + to_left.astype(F32)])
            else:
                a, b = a + to_right.astype(F32), b + to_left.astype(F32)
            first, second = a.astype(wire), b.astype(wire)
            to_right, to_left = send(first, right), send(second, left)
        mark = corner(first)
        swap(far, out, mark)
        return last(keeps[far][0], others[far][0], to_right, to_left)

    def gather(own, use, lag):
        a, b = send(own, right), send(own, left)
        came = [([(0, 0)], [own])]
        waiting = [([(1, 0)], [send(own, across)])]
        cut = own.shape[0] // 2
        for i in range(1, far):
            if not lag:
                came, waiting = came + waiting, []
            mark = use(sum([c[0] for c in came], []), sum([c[1] for c in came], []))
            came, waiting = waiting, []
            a = join(a, mark)
            places, got = [chips - i, i], [a, b]
            if i < far - 1:
                a, b = send(a, right), send(b, left)
            else:
                a, b = send(a[:cut], right), send(b[cut:], left)
            came.append(([(0, p) for p in places], got))
            waiting.append(([(1, p) for p in places], [send(piece, across) for piece in got]))
        came = came + waiting
        mark = use(sum([c[0] for c in came], []), sum([c[1] for c in came], []))
        last = jnp.concatenate([join(a, mark), b])
        return [(0, far), (1, far)], [last, send(last, across)]

    def where(items):
        return jnp.stack([index(h, i) for h, i in items]).astype(jnp.int32)

    features = basis.shape[0] * 2 * chips
    wire_scale = 2.0 ** math.floor(math.log2(60000.0 / (X_MAX * BASIS_MAX * features)))
    listed = [(h, i) for r in rounds for h in range(2) for i in r]
    x, tiles = start(where(listed), token_ids.reshape(-1, 1), hidden_pool, basis, kb)

    def projected(r):
        first = sum(2 * len(items) for items in rounds[:r])
        return lambda mark: project(first, (len(rounds[r]),) * 2, x, tiles, x if mark is None else mark)

    def rounded(keep, other, to_right, to_left):
        total = (keep[0] + other[0]) * wire_scale + to_right.astype(F32) + to_left.astype(F32)
        return (total * (1.0 / wire_scale)).astype(BF16)

    kept = [far] + rounds[1]
    held = {}

    def ahead(r, mark):
        if r >= len(kept):
            return mark
        held[kept[r]], mark = hold(where([(0, kept[r]), (1, kept[r])]), coeffs, kb, mark)
        return mark

    own = scatter_sum([projected(r) for r in range(far + 1)], F16, wire_scale, rounded, ahead)

    state = {"acc": None, "grad": None}

    def use_forward(items, blocks):
        found = dict(zip(items, blocks))
        near = [item for item in items if item[1] not in held]
        pairs = [i for i in kept if (0, i) in found and (1, i) in found]
        ordered = [found[item] for item in near] + [found[h, i] for i in pairs for h in range(2)]
        assert len(ordered) == len(items)
        state["acc"], mark = predict(where(near), coeffs, ordered, [held[i] for i in pairs], state["acc"])
        if len(held) < len(kept):
            mark = ahead(len(held), mark)
        return mark

    items, last = gather(own, use_forward, True)
    res, low, keep, out = residuals(last, held[far], targets, state["acc"])

    def backed(r):
        return lambda mark: backward(both(rounds[r]), coeffs, low, mark, kb)

    parts = [
        lambda mark: (keep, out),
        [lambda mark, i=i: backward_held([held[i]], low, mark, kb) for i in rounds[1]],
    ]
    parts += [backed(r) for r in range(2, far + 1)]
    own = scatter_sum(parts, BF16, 1.0, finish)
    xt = x.T

    def use_back(items, blocks):
        state["grad"], mark = gradient(where(items), xt, blocks, state["grad"], rank, -1.0 / tok_count)
        return mark

    use_back(*gather(own, use_back, False))
    return res, state["grad"]


def solution(mesh):
    placed = (
        P("groups", None),
        P("groups", "layer"),
        P("layer", "groups"),
        P(None, "groups", "layer"),
        P("groups", None, "layer"),
    )
    count = mesh.shape["layer"]
    body = functools.partial(staged, 4) if count == 16 else plain
    return jax.shard_map(
        body,
        mesh=mesh,
        in_specs=placed,
        out_specs=(P("groups", None, "layer"), P("layer", "groups")),
        check_vma=False,
    )
```
